256 devices in a mesh: section: 8 (over x, y_lo), tp: 32 (over y_hi, z, core).
Axes of the slice: x: 4, y: 4 (y_hi: 2, y_lo: 2; y = y_hi * 2 + y_lo), z: 8, core: 2. Of those that a mesh axis runs over, the one named last changes fastest.
Arguments:
- act_in: bfloat16 [8, 128, 4096], P('section', None, 'tp')
- grad_in: bfloat16 [8, 128, 4096], P('section', None, 'tp'), may hold values from -6 to 6
- fresh_in: bfloat16 [2, 128, 4096], P(None, None, 'tp')
- fresh_grad: bfloat16 [2, 128, 4096], P(None, None, 'tp'), may hold values from -6 to 6
- stash: bfloat16 [8, 4, 128, 4096], P('section', None, None, 'tp')
- plan: int32 [3, 8], replicated, may hold values from 0 to 3
- gain: float32 [8, 4096], P('section'), may hold values from 0.1 to 1.9
- w_gate: bfloat16 [8, 4096, 14336], P('section', None, 'tp'), may hold values from -0.09375 to 0.09375
- w_up: bfloat16 [8, 4096, 14336], P('section', None, 'tp'), may hold values from -0.09375 to 0.09375
- w_down: bfloat16 [8, 14336, 4096], P('section', 'tp'), may hold values from -0.046875 to 0.046875
Outputs:
- fwd_out: bfloat16 [8, 128, 4096], P('section', None, 'tp')
- grad_out: bfloat16 [8, 128, 4096], P('section', None, 'tp')
The draws below stay inside these ranges and needn't reach their ends.
All inputs are finite; a program needn't handle non-finite values.
Results may differ from the reference program's by a relative error of at most 0.012.
Values may be sent and summed in bfloat16 or wider, within the bound.
A program may use at most 64 MiB of HBM per device.

```python
import jax
import jax.numpy as jnp
from jax import lax

D = 4096
FF = 14336
MB = 128
TICKS = 3
SLOTS = 4
SECTIONS = 8


def rough_rows(key, shape, spread):
    k_base, k_rows, k_cols = jax.random.split(key, 3)
    base = jax.random.normal(k_base, shape, jnp.float32)
    top = jnp.log(spread) / 2.0
    rows = jnp.exp(jax.random.uniform(k_rows, shape[:-1] + (1,), jnp.float32, -top, top))
    cols = jnp.exp(jax.random.uniform(k_cols, shape[-1:], jnp.float32, -top, top))
    return jnp.clip(base * rows * cols, -60.0, 60.0)


def draw_act_in(key, part):
    key = jax.random.fold_in(key, 11)
    return rough_rows(key, (SECTIONS, MB, D), 10.0).astype(jnp.bfloat16)


def draw_fresh_in(key, part):
    key = jax.random.fold_in(key, 23)
    return rough_rows(key, (TICKS - 1, MB, D), 10.0).astype(jnp.bfloat16)


def draw_stash(key, part):
    key = jax.random.fold_in(key, 37)
    return rough_rows(key, (SECTIONS, SLOTS, MB, D), 10.0).astype(jnp.bfloat16)


def plant(entries, own_key, smallest, largest):
    extent = entries.shape
    place = [jax.random.randint(jax.random.fold_in(own_key, axis), (), 0, extent[axis]) for axis in range(len(extent))]
    entries = entries.at[tuple(place)].set(smallest)
    longest = extent.index(max(extent))
    place[longest] = (place[longest] + 1) % extent[longest]
    return entries.at[tuple(place)].set(largest)


def shard_levels(own_key, dims, cuts, least, top_value):
    level = 1.0
    for position, parts in cuts:
        draws = jax.random.uniform(jax.random.fold_in(jax.random.fold_in(own_key, 6), position), (parts,), jnp.float32, least / len(cuts), top_value / len(cuts))
        level = level * jnp.repeat(jnp.exp(draws), dims[position] // parts).reshape((-1,) + (1,) * (len(dims) - 1 - position))
    return level


def scatter_about(rng, shape, scale, reach, cuts=(), held_as=jnp.bfloat16):
    entries = scale * jax.random.normal(rng, shape, jnp.float32)
    if cuts:
        entries = entries * shard_levels(rng, shape, cuts, -0.22, 0.18)
    return jnp.clip(entries, -reach, reach).astype(held_as)


def setup_inputs(seed: int = 0) -> dict:
    key_list = jax.random.split(jax.random.key(seed), 11)
    act_in = draw_act_in(jax.random.fold_in(key_list[10], 71), 0)
    grad_in = scatter_about(key_list[1], (SECTIONS, MB, D), 1.0, 6.0, ((0, 8), (2, 32)))
    fresh_in = draw_fresh_in(jax.random.fold_in(key_list[10], 71), 0)
    fresh_grad = scatter_about(key_list[3], (TICKS - 1, MB, D), 1.0, 6.0, ((2, 32),))
    stash = draw_stash(jax.random.fold_in(key_list[10], 71), 0)
    plan = plant(jax.random.randint(key_list[5], (TICKS, SECTIONS), 0, SLOTS), jax.random.fold_in(key_list[5], 1), 0, SLOTS - 1).astype(jnp.int32)
    gain = jnp.clip(1.0 + 0.18 * jax.random.normal(key_list[6], (SECTIONS, D), jnp.float32), 0.1, 1.9)
    w_gate = scatter_about(key_list[7], (SECTIONS, D, FF), D ** -0.5, 0.09375, ((0, 8), (2, 32)))
    w_up = scatter_about(key_list[8], (SECTIONS, D, FF), D ** -0.5, 0.09375, ((0, 8), (2, 32)))
    w_down = scatter_about(key_list[9], (SECTIONS, FF, D), FF ** -0.5, 0.046875, ((0, 8), (1, 32)))
    return {"act_in": act_in, "grad_in": grad_in, "fresh_in": fresh_in, "fresh_grad": fresh_grad, "stash": stash, "plan": plan, "gain": gain, "w_gate": w_gate, "w_up": w_up, "w_down": w_down}


EPS = 1e-05

def norm_parts(x, gain):
    x32 = x.astype(jnp.float32)
    r = lax.rsqrt(lax.optimization_barrier(jnp.mean(x32 * x32, axis=-1, keepdims=True)) + EPS)
    normed = (x32 * r * gain).astype(jnp.bfloat16)
    return (x32, r, normed)

def contract_last(a, b):
    return lax.dot_general(a, b, (((1,), (1,)), ((), ())), preferred_element_type=jnp.float32)

def forward(x, gain, wg, wu, wd):
    x32, r, normed = norm_parts(x, gain)
    gate = jnp.dot(normed, wg, preferred_element_type=jnp.float32)
    up = jnp.dot(normed, wu, preferred_element_type=jnp.float32)
    hidden = (jax.nn.silu(gate) * up).astype(jnp.bfloat16)
    return (x32 + jnp.dot(hidden, wd, preferred_element_type=jnp.float32)).astype(jnp.bfloat16)

def backward(g, x, gain, wg, wu, wd):
    x32, r, normed = norm_parts(x, gain)
    gate = jnp.dot(normed, wg, preferred_element_type=jnp.float32)
    up = jnp.dot(normed, wu, preferred_element_type=jnp.float32)
    dh = contract_last(g, wd)
    sg = jax.nn.sigmoid(gate)
    dgate = (dh * up * sg * (1.0 + gate * (1.0 - sg))).astype(jnp.bfloat16)
    dup = (dh * gate * sg).astype(jnp.bfloat16)
    dn = contract_last(dgate, wg) + contract_last(dup, wu)
    inner = lax.optimization_barrier(jnp.sum(x32 * gain * dn, axis=-1, keepdims=True))
    dx = g.astype(jnp.float32) + r * gain * dn - x32 * r * r * r * inner / D
    return dx.astype(jnp.bfloat16)

def reference(act_in, grad_in, fresh_in, fresh_grad, stash, plan, gain, w_gate, w_up, w_down):
    half = SECTIONS // 2
    acts = [act_in[s] for s in range(SECTIONS)]
    grads = [grad_in[s] for s in range(SECTIONS)]
    outs_f = acts
    outs_b = grads
    for step in range(TICKS):
        if step > 0:
            acts = [fresh_in[step - 1]] + outs_f[:-1]
            grads = outs_b[1:] + [fresh_grad[step - 1]]
        outs_f = [forward(acts[s], gain[s], w_gate[s], w_up[s], w_down[s]) for s in range(SECTIONS)]
        outs_b = []
        for s in range(SECTIONS):
            held = stash[s ^ half][plan[step, s]]
            outs_b.append(backward(grads[s], held, gain[s], w_gate[s], w_up[s], w_down[s]))
    return (jnp.stack(outs_f), jnp.stack(outs_b))
```

```python
import functools

import jax
import jax.numpy as jnp
from jax import lax
from jax.experimental import pallas as pl
from jax.experimental.pallas import tpu as pltpu
from jax.sharding import PartitionSpec as P

EPS = 1e-05
MESH = pl.DeviceIdType.MESH
F32 = jnp.float32
BF16 = jnp.bfloat16
NT = (((1,), (1,)), ((), ()))
PARTS = 4


def dot(a, b):
    return jnp.dot(a, b, preferred_element_type=F32)


def dot_nt(a, b):
    return lax.dot_general(a, b, NT, preferred_element_type=F32)


def kernel(
    ticks,
    act,
    grad,
    fresh_f,
    fresh_b,
    stash,
    plan,
    gain,
    wg_hbm,
    wu_hbm,
    wd_hbm,
    out_f,
    out_b,
    wg,
    wu,
    wd,
    ag,
    picked,
    sib_out,
    sib_in,
    own,
    ring_out,
    ring_in,
    part_out,
    part_in,
    acc_g,
    acc_u,
    acc_h,
    ssq,
    hid,
    dgate,
    dup,
    cols,
    w_sem,
    first_s,
    first_r,
    stash_s,
    stash_r,
    ag_s,
    ag_r,
    agsib_s,
    agsib_r,
    rsib_s,
    rsib_r,
    rs_s,
    rs_r,
    sh_s,
    sh_r,
):
    sec = lax.axis_index("section")
    tp = lax.axis_index("tp")
    yh = tp // 16
    z = (tp // 2) % 8
    c = tp % 2
    width = gain.shape[1]

    def dev(s, y, zz):
        return (s, y * 16 + zz * 2 + c)

    sibling = (sec, yh * 16 + z * 2 + (1 - c))
    ring = (dev(sec, yh, (z + 1) % 8), dev(sec, yh, (z + 7) % 8))
    other_y = dev(sec, 1 - yh, z)
    partner = (sec + 4) % 8
    stash_to = [dev(partner, y, z) for y in range(2)]
    next_to = [dev((sec + 1) % 8, y, z) for y in range(2)]
    prev_to = [dev((sec + 7) % 8, y, z) for y in range(2)]

    def remote(src, dst, s_sem, r_sem, where):
        return pltpu.make_async_remote_copy(
            src_ref=src, dst_ref=dst, send_sem=s_sem, recv_sem=r_sem, device_id=where, device_id_type=MESH
        )

    loads = []
    for n, (src, dst) in enumerate(((wg_hbm, wg), (wu_hbm, wu), (wd_hbm, wd))):
        rows = dst.shape[0] // PARTS
        for p in range(PARTS):
            span = pl.ds(p * rows, rows)
            loads.append(pltpu.make_async_copy(src.at[0, span], dst.at[span], w_sem.at[n, p]))
    for load in loads:
        load.start()

    barrier = pltpu.get_barrier_semaphore()
    greet = [sibling, *ring, other_y, *stash_to, *next_to, *prev_to]
    for where in greet:
        pl.semaphore_signal(barrier, inc=1, device_id=where, device_id_type=MESH)
    ag[0, 0, c, z, yh] = act[0]
    ag[0, 1, c, z, yh] = grad[0]
    for t in range(ticks):
        picked[t] = stash[0, plan[t, partner]]
    pl.semaphore_wait(barrier, len(greet))

    first = []
    for q in range(2):
        mine = ag.at[0, q, c, z, yh]
        first.append(remote(mine, mine, first_s.at[q], first_r.at[q], other_y))
    for copy in first:
        copy.start()
    stashed = []
    for t in range(ticks):
        for y in range(2):
            stashed.append(
                remote(picked.at[t], ag.at[t, 2, c, z, yh], stash_s.at[t, y], stash_r.at[t, yh], stash_to[y])
            )
    for copy in stashed:
        copy.start()
    for q in range(2):
        theirs = ag.at[0, q, c, z, 1 - yh]
        remote(theirs, theirs, first_s.at[q], first_r.at[q], other_y).wait_recv()
    for load in loads:
        load.wait()

    def tick(t, _):
        sends = []

        def start(copy):
            copy.start()
            sends.append(copy)

        for y in range(2):
            slot = ag.at[t, 2, c, z, y]
            remote(slot, slot, stash_s.at[t, y], stash_r.at[t, y], stash_to[y]).wait_recv()

        def block_at(q, d, k, core):
            zz = (z + 7 - k) % 8 if d == 0 else (z + 1 + k) % 8
            if k == 3:
                return ag.at[t, q, core, zz, pl.ds(d, 1)]
            return ag.at[t, q, core, zz]

        def ring_send(q, d, k):
            zz = (z + 8 - k) % 8 if d == 0 else (z + k) % 8
            ref = ag.at[t, q, c, zz, pl.ds(d, 1)] if k == 3 else ag.at[t, q, c, zz]
            start(remote(ref, ref, ag_s.at[t, q, d, k], ag_r.at[t, q, d, k], ring[d]))

        def sib_send(q, slot, ref):
            start(remote(ref, ref, agsib_s.at[t, q, slot], agsib_r.at[t, q, slot], sibling))

        def sib_wait(q, slot, ref):
            remote(ref, ref, agsib_s.at[t, q, slot], agsib_r.at[t, q, slot], sibling).wait_recv()

        acc_g[...] = jnp.zeros_like(acc_g)
        acc_u[...] = jnp.zeros_like(acc_u)
        acc_h[...] = jnp.zeros_like(acc_h)
        ssq[...] = jnp.zeros_like(ssq)

        def wide(q, zz, y):
            return jnp.concatenate([ag[t, q, 0, zz, y], ag[t, q, 1, zz, y]], axis=1)

        def absorb(zz, y):
            at = pl.ds(pl.multiple_of((y * 8 + zz) * 256, 256), 256)
            x = jnp.concatenate([wide(0, zz, y), wide(2, zz, y)], axis=0).astype(F32)
            sq = x * x
            ssq[...] += sq[:, :128] + sq[:, 128:]
            xg = (x * gain[:, at]).astype(BF16)
            acc_g[...] += dot(xg, wg[at, :])
            acc_u[...] += dot(xg, wu[at, :])
            acc_h[...] += dot_nt(wide(1, zz, y), wd[:, at])

        for q in (0, 1, 2):
            for d in range(2):
                ring_send(q, d, 0)
            sib_send(q, 0, ag.at[t, q, c, z])
        for k in range(4):
            for q in (0, 1, 2):
                for d in range(2):
                    ref = block_at(q, d, k, c)
                    remote(ref, ref, ag_s.at[t, q, d, k], ag_r.at[t, q, d, k], ring[d]).wait_recv()
                    if k < 3:
                        ring_send(q, d, k + 1)
                    sib_send(q, 1 + 2 * k + d, ref)
            if k == 0:
                for q in range(3):
                    sib_wait(q, 0, ag.at[t, q, 1 - c, z])

                def own_blocks(j, _):
                    absorb(z, j)
                    return 0

                lax.fori_loop(0, 2, own_blocks, 0)
            else:
                for q in range(3):
                    for d in range(2):
                        sib_wait(q, 2 * k - 1 + d, block_at(q, d, k - 1, 1 - c))

                def far_blocks(j, _):
                    d = j // 2
                    absorb((z + 8 - k + 2 * k * d) % 8, j % 2)
                    return 0

                lax.fori_loop(0, 4, far_blocks, 0)
        for q in range(3):
            for d in range(2):
                sib_wait(q, 7 + d, block_at(q, d, 3, 1 - c))

        def last_blocks(j, _):
            absorb((z + 4) % 8, j)
            return 0

        lax.fori_loop(0, 2, last_blocks, 0)

        r = lax.rsqrt(jnp.sum(ssq[...], axis=1, keepdims=True) / width + EPS)

        def scaled(acc, lo):
            rr = r[lo : lo + 128]
            return jnp.where(rr > 0.0, rr * acc[lo : lo + 128, :], 0.0)

        gate_f = scaled(acc_g, 0)
        hid[...] = (gate_f * jax.nn.sigmoid(gate_f) * scaled(acc_u, 0)).astype(BF16)
        gate_b = scaled(acc_g, 128)
        up_b = scaled(acc_u, 128)
        sig = jax.nn.sigmoid(gate_b)
        grad_h = acc_h[...]
        dg = (grad_h * up_b * sig * (1.0 + gate_b * (1.0 - sig))).astype(BF16)
        du = (grad_h * gate_b * sig).astype(BF16)
        dgate[...] = dg
        dup[...] = du
        inner = jnp.sum(dg.astype(F32) * gate_b + du.astype(F32) * up_b, axis=1, keepdims=True)
        cols[0] = jnp.broadcast_to(r[128:], (128, 128))
        cols[1] = jnp.broadcast_to(inner / width, (128, 128))

        def terms(q, zz, y):
            at = pl.ds(pl.multiple_of((y * 8 + zz) * 256, 256), 256)
            if q == 0:
                return dot(hid[...], wd[:, at])
            dn = (dot_nt(dgate[...], wg[at, :]) + dot_nt(dup[...], wu[at, :])) * gain[:, at]
            rb = jnp.concatenate([cols[0], cols[0]], axis=1)
            cb = jnp.concatenate([cols[1], cols[1]], axis=1)
            return rb * (dn - wide(2, zz, y).astype(F32) * rb * cb)

        def produce(q, slot, zz):
            def one(y, _):
                value = terms(q, zz, y)
                lo, hi = value[:, :128], value[:, 128:]
                own[q, zz, y] = jnp.where(c == 0, lo, hi)
                sib_out[t, q, zz, y] = jnp.where(c == 0, hi, lo).astype(BF16)
                return 0

            lax.fori_loop(0, 2, one, 0)
            start(
                remote(sib_out.at[t, q, zz], sib_in.at[t, q, zz], rsib_s.at[t, q, slot], rsib_r.at[t, q, slot], sibling)
            )

        def dest(d, k):
            return (z + 4 - k) % 8 if d == 0 else (z + 4 + k) % 8

        def produce_step(k):
            for q in range(2):
                if k in (0, 4):
                    produce(q, 2 * k - (k > 0), dest(0, k))
                else:
                    for d in range(2):
                        produce(q, 2 * k - 1 + d, dest(d, k))

        def sib_ready(q, slot, zz):
            ref = sib_in.at[t, q, zz]
            remote(ref, ref, rsib_s.at[t, q, slot], rsib_r.at[t, q, slot], sibling).wait_recv()

        def local(q, zz, y):
            return own[q, zz, y] + sib_in[t, q, zz, y].astype(F32)

        def landing(q, d, k, ref):
            return ref.at[t, q, d, k, pl.ds(d, 1)] if k == 0 else ref.at[t, q, d, k]

        def ring_ready(q, d, k):
            ref = landing(q, d, k, ring_in)
            remote(ref, ref, rs_s.at[t, q, d, k], rs_r.at[t, q, d, k], ring[d]).wait_recv()

        produce_step(0)
        for k in range(4):
            produce_step(k + 1)
            for q in range(2):
                if k == 0:
                    sib_ready(q, 0, dest(0, 0))
                for d in range(2):
                    if k > 0:
                        sib_ready(q, 2 * k - 1 + d, dest(d, k))
                        ring_ready(q, d, k - 1)
                    for y in (d,) if k == 0 else (0, 1):
                        total = local(q, dest(d, k), y)
                        if k > 1 or (k == 1 and y == d):
                            total += ring_in[t, q, d, k - 1, y].astype(F32)
                        ring_out[t, q, d, k, y] = total.astype(BF16)
                    start(
                        remote(
                            landing(q, d, k, ring_out),
                            landing(q, d, k, ring_in),
                            rs_s.at[t, q, d, k],
                            rs_r.at[t, q, d, k],
                            ring[d],
                        )
                    )
        for q in range(2):
            sib_ready(q, 7, z)
            for d in range(2):
                ring_ready(q, d, 3)

        def summed(q, y):
            total = local(q, z, y) + ring_in[t, q, 0, 3, y].astype(F32) + ring_in[t, q, 1, 3, y].astype(F32)
            return total + jnp.where(y == yh, ag[t, q, c, z, yh].astype(F32), 0.0)

        @pl.when(t < ticks - 1)
        def _():
            moves = []
            for q, edge, fresh, to in ((0, 7, fresh_f, next_to), (1, 0, fresh_b, prev_to)):
                for y in range(2):
                    new = jnp.where(y == yh, fresh[t].astype(F32), 0.0)
                    part_out[t, q, y] = jnp.where(sec == edge, new, summed(q, y)).astype(BF16)
                for y in range(2):
                    copy = remote(
                        part_out.at[t, q], part_in.at[t, q, yh], sh_s.at[t, q, y], sh_r.at[t, q, yh], to[y]
                    )
                    copy.start()
                    moves.append(copy)
            for copy in sends:
                copy.wait_send()
            for q, to in ((0, next_to), (1, prev_to)):
                for y in range(2):
                    ref = part_in.at[t, q, y]
                    remote(ref, ref, sh_s.at[t, q, y], sh_r.at[t, q, y], to[y]).wait_recv()
                for y in range(2):
                    ag[t + 1, q, c, z, y] = (
                        part_in[t, q, 0, y].astype(F32) + part_in[t, q, 1, y].astype(F32)
                    ).astype(BF16)
            for copy in moves:
                copy.wait_send()

        @pl.when(t == ticks - 1)
        def _():
            moves = []
            for q in range(2):
                part_out[t, q, 1 - yh] = summed(q, 1 - yh).astype(BF16)
                copy = remote(
                    part_out.at[t, q, 1 - yh],
                    part_in.at[t, q, yh, 1 - yh],
                    sh_s.at[t, q, 0],
                    sh_r.at[t, q, yh],
                    other_y,
                )
                copy.start()
                moves.append(copy)
            for copy in sends:
                copy.wait_send()
            for q, out in ((0, out_f), (1, out_b)):
                ref = part_in.at[t, q, 1 - yh, yh]
                remote(ref, ref, sh_s.at[t, q, 0], sh_r.at[t, q, 1 - yh], other_y).wait_recv()
                out[0] = (summed(q, yh) + part_in[t, q, 1 - yh, yh].astype(F32)).astype(BF16)
            for copy in moves:
                copy.wait_send()

        return 0

    lax.fori_loop(0, ticks, tick, 0)
    for copy in first + stashed:
        copy.wait_send()


def on_device(act_in, grad_in, fresh_in, fresh_grad, stash, plan, gain, w_gate, w_up, w_down):
    ticks = plan.shape[0]
    rows, cols = act_in.shape[1:]
    width, units = w_gate.shape[1:]
    tile = (rows, cols)
    vmem = pl.BlockSpec(memory_space=pltpu.VMEM)
    anywhere = pl.BlockSpec(memory_space=pl.ANY)
    dma = pltpu.SemaphoreType.DMA
    return pl.pallas_call(
        functools.partial(kernel, ticks),
        out_shape=[jax.ShapeDtypeStruct((1,) + tile, BF16)] * 2,
        in_specs=[vmem] * 5 + [pl.BlockSpec(memory_space=pltpu.SMEM), vmem] + [anywhere] * 3,
        out_specs=[vmem] * 2,
        scratch_shapes=[
            pltpu.VMEM((width, units), BF16),
            pltpu.VMEM((width, units), BF16),
            pltpu.VMEM((units, width), BF16),
            pltpu.VMEM((ticks, 3, 2, 8, 2) + tile, BF16),
            pltpu.VMEM((ticks,) + tile, BF16),
            pltpu.VMEM((ticks, 2, 8, 2) + tile, BF16),
            pltpu.VMEM((ticks, 2, 8, 2) + tile, BF16),
            pltpu.VMEM((2, 8, 2) + tile, F32),
            pltpu.VMEM((ticks, 2, 2, 4, 2) + tile, BF16),
            pltpu.VMEM((ticks, 2, 2, 4, 2) + tile, BF16),
            pltpu.VMEM((ticks, 2, 2) + tile, BF16),
            pltpu.VMEM((ticks, 2, 2, 2) + tile, BF16),
            pltpu.VMEM((2 * rows, units), F32),
            pltpu.VMEM((2 * rows, units), F32),
            pltpu.VMEM((rows, units), F32),
            pltpu.VMEM((2 * rows, 128), F32),
            pltpu.VMEM((rows, units), BF16),
            pltpu.VMEM((rows, units), BF16),
            pltpu.VMEM((rows, units), BF16),
            pltpu.VMEM((2, rows, 128), F32),
            dma((3, PARTS)),
            dma((2,)),
            dma((2,)),
            dma((ticks, 2)),
            dma((ticks, 2)),
            dma((ticks, 3, 2, 4)),
            dma((ticks, 3, 2, 4)),
            dma((ticks, 3, 9)),
            dma((ticks, 3, 9)),
            dma((ticks, 2, 8)),
            dma((ticks, 2, 8)),
            dma((ticks, 2, 2, 4)),
            dma((ticks, 2, 2, 4)),
            dma((ticks, 2, 2)),
            dma((ticks, 2, 2)),
        ],
        compiler_params=pltpu.CompilerParams(
            collective_id=0, has_side_effects=True, vmem_limit_bytes=56 * 2**20
        ),
        name="relay",
    )(act_in, grad_in, fresh_in, fresh_grad, stash, plan, gain, w_gate, w_up, w_down)


def solution(mesh):
    in_specs = (
        P("section", None, "tp"),
        P("section", None, "tp"),
        P(None, None, "tp"),
        P(None, None, "tp"),
        P("section", None, None, "tp"),
        P(),
        P("section", None),
        P("section", None, "tp"),
        P("section", None, "tp"),
        P("section", "tp", None),
    )
    out_specs = (P("section", None, "tp"), P("section", None, "tp"))
    return jax.shard_map(on_device, mesh=mesh, in_specs=in_specs, out_specs=out_specs, check_vma=False)
```

```python
import functools

import jax
import jax.numpy as jnp
from jax import lax
from jax.experimental import pallas as pl
from jax.experimental.pallas import tpu as pltpu
from jax.sharding import PartitionSpec as P

EPS = 1e-05
MESH = pl.DeviceIdType.MESH
F32 = jnp.float32
BF16 = jnp.bfloat16
NT = (((1,), (1,)), ((), ()))
PARTS = 4


def dot(a, b):
    return jnp.dot(a, b, preferred_element_type=F32)


def dot_nt(a, b):
    return lax.dot_general(a, b, NT, preferred_element_type=F32)


def kernel(
    ticks,
    act,
    grad,
    fresh_f,
    fresh_b,
    stash,
    plan,
    gain,
    wg_hbm,
    wu_hbm,
    wd_hbm,
    outs,
    wgu,
    wd,
    ag,
    sg,
    picked,
    sib_out,
    sib_in,
    own,
    ring_out,
    ring_in,
    part_out,
    part_in,
    acc_g,
    acc_u,
    acc_h,
    ssq,
    hid,
    dgu,
    cols,
    w_sem,
    first_s,
    first_r,
    stash_s,
    stash_r,
    spread_s,
    spread_r,
    cross_s,
    cross_r,
    pair_s,
    pair_r,
    ag_s,
    ag_r,
    agsib_s,
    agsib_r,
    rsib_s,
    rsib_r,
    rs_s,
    rs_r,
    sh_s,
    sh_r,
):
    sec = lax.axis_index("section")
    tp = lax.axis_index("tp")
    yh = tp // 16
    z = (tp // 2) % 8
    c = tp % 2
    width = gain.shape[1]

    def dev(s, y, zz):
        return (s, y * 16 + zz * 2 + c)

    sibling = (sec, yh * 16 + z * 2 + (1 - c))
    ring = (dev(sec, yh, (z + 1) % 8), dev(sec, yh, (z + 7) % 8))
    other_y = dev(sec, 1 - yh, z)
    partner = (sec + 4) % 8
    stash_to = dev(partner, yh, z)
    along = [dev(sec, yh, (z + i) % 8) for i in range(1, 8)]
    next_to = [dev((sec + 1) % 8, y, z) for y in range(2)]
    prev_to = [dev((sec + 7) % 8, y, z) for y in range(2)]

    def remote(src, dst, s_sem, r_sem, where):
        return pltpu.make_async_remote_copy(
            src_ref=src, dst_ref=dst, send_sem=s_sem, recv_sem=r_sem, device_id=where, device_id_type=MESH
        )

    loads = []
    units = wd.shape[0]
    rows = units // PARTS
    for n, (src, dst, base) in enumerate(((wg_hbm, wgu, 0), (wu_hbm, wgu, units), (wd_hbm, wd, 0))):
        for p in range(PARTS):
            span = pl.ds(p * rows, rows)
            loads.append(pltpu.make_async_copy(src.at[0, span], dst.at[pl.ds(base + p * rows, rows)], w_sem.at[n, p]))
    for load in loads:
        load.start()

    barrier = pltpu.get_barrier_semaphore()
    greet = [sibling, *along, other_y, stash_to, *next_to, *prev_to]
    for where in greet:
        pl.semaphore_signal(barrier, inc=1, device_id=where, device_id_type=MESH)
    ag[0, 0, c, z, yh] = act[0]
    ag[0, 1, c, z, yh] = grad[0]
    for t in range(ticks):
        picked[t] = stash[0, plan[t, partner]]
    pl.semaphore_wait(barrier, len(greet))

    first = []
    for q in range(2):
        mine = ag.at[0, q, c, z, yh]
        first.append(remote(mine, mine, first_s.at[q], first_r.at[q], other_y))
    for copy in first:
        copy.start()
    stashed = [remote(picked.at[t], sg.at[t, c, yh, z], stash_s.at[t], stash_r.at[t], stash_to) for t in range(ticks)]
    for copy in stashed:
        copy.start()

    def stash_ready(t):
        ref = sg.at[t, c, yh, z]
        remote(ref, ref, stash_s.at[t], stash_r.at[t], stash_to).wait_recv()

    def spread(t, i, zz):
        ref = sg.at[t, c, yh, zz]
        return remote(ref, ref, spread_s.at[t, i], spread_r.at[t, i], along[i])

    def spread_start(t):
        stash_ready(t)
        for i in (3, 4, 2, 5, 1, 6, 0):
            spread(t, i, z).start()

    def cross(t, y):
        ref = sg.at[t, c, y]
        return remote(ref, ref, cross_s.at[t], cross_r.at[t], other_y)

    def cross_start(t):
        for i in range(7):
            spread(t, i, (z + 7 - i) % 8).wait_recv()
        cross(t, yh).start()

    def pair(t, core):
        ref = sg.at[t, core]
        return remote(ref, ref, pair_s.at[t], pair_r.at[t], sibling)

    def pair_start(t):
        cross(t, 1 - yh).wait_recv()
        pair(t, c).start()

    def spread_sent(t):
        for i in range(7):
            spread(t, i, z).wait_send()
        cross(t, yh).wait_send()


    def first_ready(q):
        theirs = ag.at[0, q, c, z, 1 - yh]
        remote(theirs, theirs, first_s.at[q], first_r.at[q], other_y).wait_recv()

    def f_move(t, y, source):
        return remote(part_out.at[t, 0], part_in.at[t, 0, source], sh_s.at[t, 0, y], sh_r.at[t, 0, source], next_to[y])

    def b_move(t, y, source):
        return remote(part_out.at[t, 1], part_in.at[t, 1, source], sh_s.at[t, 1, y], sh_r.at[t, 1, source], prev_to[y])

    def tick(t, _):
        sends = []

        def start(copy):
            copy.start()
            sends.append(copy)

        def behind(d, k):
            return (z + 8 - k) % 8 if d == 0 else (z + k) % 8

        def halves(k, d):
            return (d,) if k == 3 else (0, 1)

        def ring_copy(q, d, k, y, zz):
            ref = ag.at[t, q, c, zz, y]
            return remote(ref, ref, ag_s.at[t, q, d, k, y], ag_r.at[t, q, d, k, y], ring[d])

        def sib_copy(q, slot, zz, core):
            ref = ag.at[t, q, core, zz]
            return remote(ref, ref, agsib_s.at[t, q, slot], agsib_r.at[t, q, slot], sibling)

        def sib_wait(slot, zz):
            for q in range(2):
                sib_copy(q, slot, zz, 1 - c).wait_recv()

        def leave(q):
            for d in range(2):
                start(ring_copy(q, d, 0, yh, z))
            pl.when(t == 0)(lambda: first_ready(q))
            for d in range(2):
                start(ring_copy(q, d, 0, 1 - yh, z))
            start(sib_copy(q, 0, z, c))

        @pl.when(t > 0)
        def _():
            f_move(t - 1, 0, 0).wait_recv()
            f_move(t - 1, 1, 1).wait_recv()
            for y in range(2):
                both = part_in[t - 1, 0, 0, y].astype(F32) + part_in[t - 1, 0, 1, y].astype(F32)
                ag[t, 0, c, z, y] = both.astype(BF16)

        leave(0)

        @pl.when(t > 0)
        def _():
            b_move(t - 1, 0, 0).wait_recv()
            b_move(t - 1, 1, 1).wait_recv()
            for y in range(2):
                both = part_in[t - 1, 1, 0, y].astype(F32) + part_in[t - 1, 1, 1, y].astype(F32)
                ag[t, 1, c, z, y] = both.astype(BF16)

        leave(1)

        acc_g[...] = jnp.zeros_like(acc_g)
        acc_u[...] = jnp.zeros_like(acc_u)
        acc_h[...] = jnp.zeros_like(acc_h)
        ssq[...] = jnp.zeros_like(ssq)

        def wide(q, zz, y):
            return jnp.concatenate([ag[t, q, 0, zz, y], ag[t, q, 1, zz, y]], axis=1)

        def held(zz, y):
            return jnp.concatenate([sg[t, 0, y, zz], sg[t, 1, y, zz]], axis=1)

        def enter(lo, block, zz, also):
            rows = pl.ds(lo, 128)
            g_sum, u_sum, h_sum, q_sum = 0.0, 0.0, 0.0, 0.0
            for y in range(2):
                at = pl.ds(pl.multiple_of((y * 8 + zz) * 256, 256), 256)
                x = block(zz, y).astype(F32)
                sq = x * x
                q_sum += sq[:, :128] + sq[:, 128:]
                xg = (x * gain[:, at]).astype(BF16)
                g_sum += dot_nt(xg, wgu[:units, at])
                u_sum += dot_nt(xg, wgu[units:, at])
                if also:
                    h_sum += dot_nt(wide(1, zz, y), wd[:, at])
            ssq[rows, :] += q_sum
            acc_g[rows, :] += g_sum
            acc_u[rows, :] += u_sum
            if also:
                acc_h[...] += h_sum

        def absorb(zz):
            enter(0, functools.partial(wide, 0), zz, True)

        def absorb_held(first, count):
            def one(j, _):
                enter(128, held, (z + j) % 8, False)
                return 0

            lax.fori_loop(first, first + count, one, 0)

        @pl.when(t == 0)
        def _():
            spread_start(0)
            for load in loads:
                load.wait()

        @pl.when(t > 0)
        def _():
            f_move(t - 1, 0, 0).wait_send()
            f_move(t - 1, 1, 0).wait_send()
            b_move(t - 1, 0, 0).wait_send()
            b_move(t - 1, 1, 0).wait_send()
            pair(t, c).wait_send()
            pair(t, 1 - c).wait_recv()
            absorb_held(0, 3)

        sib_wait(0, z)

        def arrivals(q, k):
            for y in range(2):
                for d in range(2):
                    if y in halves(k, d):
                        zz = behind(d, k + 1)
                        ring_copy(q, d, k, y, zz).wait_recv()
                        if k < 3 and y in halves(k + 1, d):
                            start(ring_copy(q, d, k + 1, y, zz))
            if k == 3:
                start(sib_copy(q, 7, (z + 4) % 8, c))
            else:
                for d in range(2):
                    start(sib_copy(q, 1 + 2 * k + d, behind(d, k + 1), c))

        for k in range(4):
            for q in range(2):
                arrivals(q, k)
                if k > 0:
                    sib_wait(2 * k - 1 + q, behind(q, k))
                    absorb(behind(q, k))
                elif q == 0:
                    absorb(z)
                else:

                    @pl.when(t > 0)
                    def _():
                        absorb_held(3, 5)

            if k == 1:
                pl.when(t == 0)(lambda: cross_start(0))
            if k == 3:
                pl.when(t == 0)(lambda: pair_start(0))
        pl.when(t < ticks - 1)(lambda: spread_start(t + 1))
        sib_wait(7, (z + 4) % 8)
        absorb((z + 4) % 8)

        def scaled(lo):
            rows = pl.ds(lo, 128)
            r = lax.rsqrt(jnp.sum(ssq[rows, :], axis=1, keepdims=True) / width + EPS)
            gate = jnp.where(r > 0.0, r * acc_g[rows, :], 0.0)
            up = jnp.where(r > 0.0, r * acc_u[rows, :], 0.0)
            return r, gate, up

        def hidden_forward():
            _, gate, up = scaled(0)
            hid[...] = (gate * jax.nn.sigmoid(gate) * up).astype(BF16)

        def hidden_backward():
            r, gate, up = scaled(128)
            sig = jax.nn.sigmoid(gate)
            grad_h = acc_h[...]
            dg = (grad_h * up * sig * (1.0 + gate * (1.0 - sig))).astype(BF16)
            du = (grad_h * gate * sig).astype(BF16)
            dgu[...] = jnp.concatenate([dg, du], axis=1)
            inner = jnp.sum(dg.astype(F32) * gate + du.astype(F32) * up, axis=1, keepdims=True)
            cols[0] = jnp.broadcast_to(r, (128, 128))
            cols[1] = jnp.broadcast_to(inner / width, (128, 128))

        def terms(q, zz, y):
            at = pl.ds(pl.multiple_of((y * 8 + zz) * 256, 256), 256)
            if q == 0:
                return dot(hid[...], wd[:, at])
            dn = dot(dgu[...], wgu[:, at]) * gain[:, at]
            rb = jnp.concatenate([cols[0], cols[0]], axis=1)
            cb = jnp.concatenate([cols[1], cols[1]], axis=1)
            return rb * (dn - held(zz, y).astype(F32) * rb * cb)

        def produce(q, slot, zz):
            def one(y, _):
                value = terms(q, zz, y)
                lo, hi = value[:, :128], value[:, 128:]
                own[q, zz, y] = jnp.where(c == 0, lo, hi)
                sib_out[t, q, zz, y] = jnp.where(c == 0, hi, lo).astype(BF16)
                return 0

            lax.fori_loop(0, 2, one, 0)
            start(
                remote(sib_out.at[t, q, zz], sib_in.at[t, q, zz], rsib_s.at[t, q, slot], rsib_r.at[t, q, slot], sibling)
            )

        def dest(d, k):
            return (z + 4 - k) % 8 if d == 0 else (z + 4 + k) % 8

        def produce_step(q, k):
            if k in (0, 4):
                produce(q, 2 * k - (k > 0), dest(0, k))
            else:
                for d in range(2):
                    produce(q, 2 * k - 1 + d, dest(d, k))

        def sib_ready(q, slot, zz):
            ref = sib_in.at[t, q, zz]
            remote(ref, ref, rsib_s.at[t, q, slot], rsib_r.at[t, q, slot], sibling).wait_recv()

        def local(q, zz, y):
            return own[q, zz, y] + sib_in[t, q, zz, y].astype(F32)

        def ring_sum(q, d, k, y):
            return remote(
                ring_out.at[t, q, d, k, y],
                ring_in.at[t, q, d, k, y],
                rs_s.at[t, q, d, k, y],
                rs_r.at[t, q, d, k, y],
                ring[d],
            )

        def pass_on(q, k):
            if k == 0:
                sib_ready(q, 0, dest(0, 0))
            else:
                for d in range(2):
                    sib_ready(q, 2 * k - 1 + d, dest(d, k))
            for y in range(2):
                for d in range(2):
                    if k == 0 and y != d:
                        continue
                    total = local(q, dest(d, k), y)
                    if k > 1 or (k == 1 and y == d):
                        ring_sum(q, d, k - 1, y).wait_recv()
                        total += ring_in[t, q, d, k - 1, y].astype(F32)
                    ring_out[t, q, d, k, y] = total.astype(BF16)
                    start(ring_sum(q, d, k, y))

        hidden_forward()
        produce_step(0, 0)

        @pl.when(t == 0)
        def _():
            pair(0, 1 - c).wait_recv()
            pair(0, c).wait_send()
            absorb_held(0, 8)

        hidden_backward()
        produce_step(1, 0)
        for k in range(4):
            for q in range(2):
                pass_on(q, k)
                produce_step(q, k + 1)
            if k == 1:
                pl.when(t < ticks - 1)(lambda: cross_start(t + 1))

        def finish(q):
            sib_ready(q, 7, z)
            for y in range(2):
                for d in range(2):
                    ring_sum(q, d, 3, y).wait_recv()

        def summed(q, y):
            total = local(q, z, y) + ring_in[t, q, 0, 3, y].astype(F32) + ring_in[t, q, 1, 3, y].astype(F32)
            return total + jnp.where(y == yh, ag[t, q, c, z, yh].astype(F32), 0.0)

        @pl.when(t < ticks - 1)
        def _():
            for q, edge, fresh, move in ((0, 7, fresh_f, f_move), (1, 0, fresh_b, b_move)):
                finish(q)
                for y in range(2):
                    new = jnp.where(y == yh, fresh[t].astype(F32), 0.0)
                    part_out[t, q, y] = jnp.where(sec == edge, new, summed(q, y)).astype(BF16)
                for y in range(2):
                    move(t, y, yh).start()
            pair_start(t + 1)
            for copy in sends:
                copy.wait_send()
            spread_sent(t + 1)

        @pl.when(t == ticks - 1)
        def _():
            moves = []
            for q in range(2):
                finish(q)
                part_out[t, q, 1 - yh] = summed(q, 1 - yh).astype(BF16)
                copy = remote(
                    part_out.at[t, q, 1 - yh],
                    part_in.at[t, q, yh, 1 - yh],
                    sh_s.at[t, q, 0],
                    sh_r.at[t, q, yh],
                    other_y,
                )
                copy.start()
                moves.append(copy)
            for copy in sends:
                copy.wait_send()
            for q in range(2):
                ref = part_in.at[t, q, 1 - yh, yh]
                remote(ref, ref, sh_s.at[t, q, 0], sh_r.at[t, q, 1 - yh], other_y).wait_recv()
                outs[q] = (summed(q, yh) + part_in[t, q, 1 - yh, yh].astype(F32)).astype(BF16)
            for copy in moves:
                copy.wait_send()

        return 0

    lax.fori_loop(0, ticks, tick, 0)
    for copy in first + stashed:
        copy.wait_send()
    spread_sent(0)


def on_device(act_in, grad_in, fresh_in, fresh_grad, stash, plan, gain, w_gate, w_up, w_down):
    ticks = plan.shape[0]
    rows, cols = act_in.shape[1:]
    width, units = w_gate.shape[1:]
    tile = (rows, cols)
    vmem = pl.BlockSpec(memory_space=pltpu.VMEM)
    anywhere = pl.BlockSpec(memory_space=pl.ANY)
    dma = pltpu.SemaphoreType.DMA
    both = pl.pallas_call(
        functools.partial(kernel, ticks),
        out_shape=jax.ShapeDtypeStruct((2,) + tile, BF16),
        in_specs=[vmem] * 5 + [pl.BlockSpec(memory_space=pltpu.SMEM), vmem] + [anywhere] * 3,
        out_specs=vmem,
        scratch_shapes=[
            pltpu.VMEM((2 * units, width), BF16),
            pltpu.VMEM((units, width), BF16),
            pltpu.VMEM((ticks, 2, 2, 8, 2) + tile, BF16),
            pltpu.VMEM((ticks, 2, 2, 8) + tile, BF16),
            pltpu.VMEM((ticks,) + tile, BF16),
            pltpu.VMEM((ticks, 2, 8, 2) + tile, BF16),
            pltpu.VMEM((ticks, 2, 8, 2) + tile, BF16),
            pltpu.VMEM((2, 8, 2) + tile, F32),
            pltpu.VMEM((ticks, 2, 2, 4, 2) + tile, BF16),
            pltpu.VMEM((ticks, 2, 2, 4, 2) + tile, BF16),
            pltpu.VMEM((ticks, 2, 2) + tile, BF16),
            pltpu.VMEM((ticks, 2, 2, 2) + tile, BF16),
            pltpu.VMEM((2 * rows, units), F32),
            pltpu.VMEM((2 * rows, units), F32),
            pltpu.VMEM((rows, units), F32),
            pltpu.VMEM((2 * rows, 128), F32),
            pltpu.VMEM((rows, units), BF16),
            pltpu.VMEM((rows, 2 * units), BF16),
            pltpu.VMEM((2, rows, 128), F32),
            dma((3, PARTS)),
            dma((2,)),
            dma((2,)),
            dma((ticks,)),
            dma((ticks,)),
            dma((ticks, 7)),
            dma((ticks, 7)),
            dma((ticks,)),
            dma((ticks,)),
            dma((ticks,)),
            dma((ticks,)),
            dma((ticks, 2, 2, 4, 2)),
            dma((ticks, 2, 2, 4, 2)),
            dma((ticks, 2, 8)),
            dma((ticks, 2, 8)),
            dma((ticks, 2, 8)),
            dma((ticks, 2, 8)),
            dma((ticks, 2, 2, 4, 2)),
            dma((ticks, 2, 2, 4, 2)),
            dma((ticks, 2, 2)),
            dma((ticks, 2, 2)),
        ],
        compiler_params=pltpu.CompilerParams(
            collective_id=0, has_side_effects=True, vmem_limit_bytes=56 * 2**20
        ),
        name="relay",
    )(act_in, grad_in, fresh_in, fresh_grad, stash, plan, gain, jnp.swapaxes(w_gate, 1, 2), jnp.swapaxes(w_up, 1, 2), w_down)
    return both[:1], both[1:]


def solution(mesh):
    in_specs = (
        P("section", None, "tp"),
        P("section", None, "tp"),
        P(None, None, "tp"),
        P(None, None, "tp"),
        P("section", None, None, "tp"),
        P(),
        P("section", None),
        P("section", None, "tp"),
        P("section", None, "tp"),
        P("section", "tp", None),
    )
    out_specs = (P("section", None, "tp"), P("section", None, "tp"))
    return jax.shard_map(on_device, mesh=mesh, in_specs=in_specs, out_specs=out_specs, check_vma=False)
```

```python
import functools

import jax
import jax.numpy as jnp
from jax import lax
from jax.experimental import pallas as pl
from jax.experimental.pallas import tpu as pltpu
from jax.sharding import PartitionSpec as P

EPS = 1e-05
MESH = pl.DeviceIdType.MESH
F32 = jnp.float32
BF16 = jnp.bfloat16
NT = (((1,), (1,)), ((), ()))
PARTS = 4


def dot(a, b):
    return jnp.dot(a, b, preferred_element_type=F32)


def dot_nt(a, b):
    return lax.dot_general(a, b, NT, preferred_element_type=F32)


def kernel(
    ticks,
    act,
    grad,
    fresh_f_hbm,
    fresh_b_hbm,
    stash_hbm,
    plan,
    gain_hbm,
    wg_hbm,
    wu_hbm,
    wd_hbm,
    outs,
    fresh_f,
    fresh_b,
    stash,
    gain,
    small_sem,
    wgu,
    wd,
    ag,
    sg,
    picked,
    sib_out,
    sib_in,
    own,
    ring_out,
    ring_in,
    part_out,
    part_in,
    acc_g,
    acc_u,
    acc_h,
    ssq,
    hid,
    dgu,
    cols,
    w_sem,
    first_s,
    first_r,
    stash_s,
    stash_r,
    spread_s,
    spread_r,
    cross_s,
    cross_r,
    pair_s,
    pair_r,
    ag_s,
    ag_r,
    agsib_s,
    agsib_r,
    rsib_s,
    rsib_r,
    rs_s,
    rs_r,
    sh_s,
    sh_r,
):
    sec = lax.axis_index("section")
    tp = lax.axis_index("tp")
    yh = tp // 16
    z = (tp // 2) % 8
    c = tp % 2
    width = gain.shape[1]

    def dev(s, y, zz):
        return (s, y * 16 + zz * 2 + c)

    sibling = (sec, yh * 16 + z * 2 + (1 - c))
    ring = (dev(sec, yh, (z + 1) % 8), dev(sec, yh, (z + 7) % 8))
    other_y = dev(sec, 1 - yh, z)
    partner = (sec + 4) % 8
    stash_to = dev(partner, yh, z)
    along = [dev(sec, yh, (z + i) % 8) for i in range(1, 8)]
    next_to = [dev((sec + 1) % 8, y, z) for y in range(2)]
    prev_to = [dev((sec + 7) % 8, y, z) for y in range(2)]

    def remote(src, dst, s_sem, r_sem, where):
        return pltpu.make_async_remote_copy(
            src_ref=src, dst_ref=dst, send_sem=s_sem, recv_sem=r_sem, device_id=where, device_id_type=MESH
        )

    smalls = [
        pltpu.make_async_copy(src, dst, small_sem.at[n])
        for n, (src, dst) in enumerate(
            (
                (act.at[0], ag.at[0, 0, c, z, yh]),
                (grad.at[0], ag.at[0, 1, c, z, yh]),
                (stash_hbm.at[0], stash),
                (fresh_f_hbm, fresh_f),
                (fresh_b_hbm, fresh_b),
                (gain_hbm, gain),
            )
        )
    ]
    for copy in smalls:
        copy.start()

    loads = []
    units = wd.shape[0]
    rows = units // PARTS
    for n, (src, dst, base) in enumerate(((wg_hbm, wgu, 0), (wu_hbm, wgu, units), (wd_hbm, wd, 0))):
        for p in range(PARTS):
            span = pl.ds(p * rows, rows)
            loads.append(pltpu.make_async_copy(src.at[0, span], dst.at[pl.ds(base + p * rows, rows)], w_sem.at[n, p]))
    for load in loads:
        load.start()

    barrier = pltpu.get_barrier_semaphore()
    greet = [sibling, *along, other_y, stash_to, *next_to, *prev_to]
    for where in greet:
        pl.semaphore_signal(barrier, inc=1, device_id=where, device_id_type=MESH)
    for copy in smalls:
        copy.wait()
    for t in range(ticks):
        picked[t] = stash[plan[t, partner]]
    pl.semaphore_wait(barrier, len(greet))

    first = []
    for q in range(2):
        mine = ag.at[0, q, c, z, yh]
        first.append(remote(mine, mine, first_s.at[q], first_r.at[q], other_y))
    for copy in first:
        copy.start()
    stashed = [remote(picked.at[t], sg.at[t, c, yh, z], stash_s.at[t], stash_r.at[t], stash_to) for t in range(ticks)]
    for copy in stashed:
        copy.start()

    def stash_ready(t):
        ref = sg.at[t, c, yh, z]
        remote(ref, ref, stash_s.at[t], stash_r.at[t], stash_to).wait_recv()

    def spread(t, i, zz):
        ref = sg.at[t, c, yh, zz]
        return remote(ref, ref, spread_s.at[t, i], spread_r.at[t, i], along[i])

    def spread_start(t):
        stash_ready(t)
        for i in (3, 4, 2, 5, 1, 6, 0):
            spread(t, i, z).start()

    def cross(t, y):
        ref = sg.at[t, c, y]
        return remote(ref, ref, cross_s.at[t], cross_r.at[t], other_y)

    def cross_start(t):
        for i in range(7):
            spread(t, i, (z + 7 - i) % 8).wait_recv()
        cross(t, yh).start()

    def pair(t, core):
        ref = sg.at[t, core]
        return remote(ref, ref, pair_s.at[t], pair_r.at[t], sibling)

    def pair_start(t):
        cross(t, 1 - yh).wait_recv()
        pair(t, c).start()

    def spread_sent(t):
        for i in range(7):
            spread(t, i, z).wait_send()
        cross(t, yh).wait_send()


    def first_ready(q):
        theirs = ag.at[0, q, c, z, 1 - yh]
        remote(theirs, theirs, first_s.at[q], first_r.at[q], other_y).wait_recv()

    def f_move(t, y, source):
        return remote(part_out.at[t, 0], part_in.at[t, 0, source], sh_s.at[t, 0, y], sh_r.at[t, 0, source], next_to[y])

    def b_move(t, y, source):
        return remote(part_out.at[t, 1], part_in.at[t, 1, source], sh_s.at[t, 1, y], sh_r.at[t, 1, source], prev_to[y])

    def tick(t, _):
        sends = []

        def start(copy):
            copy.start()
            sends.append(copy)

        def behind(d, k):
            return (z + 8 - k) % 8 if d == 0 else (z + k) % 8

        def halves(k, d):
            return (d,) if k == 3 else (0, 1)

        def ring_copy(q, d, k, y, zz):
            ref = ag.at[t, q, c, zz, y]
            return remote(ref, ref, ag_s.at[t, q, d, k, y], ag_r.at[t, q, d, k, y], ring[d])

        def sib_copy(q, slot, zz, core):
            ref = ag.at[t, q, core, zz]
            return remote(ref, ref, agsib_s.at[t, q, slot], agsib_r.at[t, q, slot], sibling)

        def sib_wait(slot, zz):
            for q in range(2):
                sib_copy(q, slot, zz, 1 - c).wait_recv()

        def leave(q):
            for d in range(2):
                start(ring_copy(q, d, 0, yh, z))
            pl.when(t == 0)(lambda: first_ready(q))
            for d in range(2):
                start(ring_copy(q, d, 0, 1 - yh, z))
            start(sib_copy(q, 0, z, c))

        @pl.when(t > 0)
        def _():
            f_move(t - 1, 0, 0).wait_recv()
            f_move(t - 1, 1, 1).wait_recv()
            for y in range(2):
                both = part_in[t - 1, 0, 0, y].astype(F32) + part_in[t - 1, 0, 1, y].astype(F32)
                ag[t, 0, c, z, y] = both.astype(BF16)

        leave(0)

        @pl.when(t > 0)
        def _():
            b_move(t - 1, 0, 0).wait_recv()
            b_move(t - 1, 1, 1).wait_recv()
            for y in range(2):
                both = part_in[t - 1, 1, 0, y].astype(F32) + part_in[t - 1, 1, 1, y].astype(F32)
                ag[t, 1, c, z, y] = both.astype(BF16)

        leave(1)

        acc_g[...] = jnp.zeros_like(acc_g)
        acc_u[...] = jnp.zeros_like(acc_u)
        acc_h[...] = jnp.zeros_like(acc_h)
        ssq[...] = jnp.zeros_like(ssq)

        def wide(q, zz, y):
            return jnp.concatenate([ag[t, q, 0, zz, y], ag[t, q, 1, zz, y]], axis=1)

        def held(zz, y):
            return jnp.concatenate([sg[t, 0, y, zz], sg[t, 1, y, zz]], axis=1)

        def enter(lo, block, zz, also):
            rows = pl.ds(lo, 128)
            g_sum, u_sum, h_sum, q_sum = 0.0, 0.0, 0.0, 0.0
            for y in range(2):
                at = pl.ds(pl.multiple_of((y * 8 + zz) * 256, 256), 256)
                x = block(zz, y).astype(F32)
                sq = x * x
                q_sum += sq[:, :128] + sq[:, 128:]
                xg = (x * gain[:, at]).astype(BF16)
                g_sum += dot_nt(xg, wgu[:units, at])
                u_sum += dot_nt(xg, wgu[units:, at])
                if also:
                    h_sum += dot_nt(wide(1, zz, y), wd[:, at])
            ssq[rows, :] += q_sum
            acc_g[rows, :] += g_sum
            acc_u[rows, :] += u_sum
            if also:
                acc_h[...] += h_sum

        def absorb(zz):
            enter(0, functools.partial(wide, 0), zz, True)

        def absorb_held(first, count):
            def one(j, _):
                enter(128, held, (z + j) % 8, False)
                return 0

            lax.fori_loop(first, first + count, one, 0)

        @pl.when(t == 0)
        def _():
            spread_start(0)
            for load in loads:
                load.wait()

        @pl.when(t > 0)
        def _():
            f_move(t - 1, 0, 0).wait_send()
            f_move(t - 1, 1, 0).wait_send()
            b_move(t - 1, 0, 0).wait_send()
            b_move(t - 1, 1, 0).wait_send()
            pair(t, c).wait_send()
            pair(t, 1 - c).wait_recv()
            absorb_held(0, 3)

        sib_wait(0, z)

        def arrivals(q, k):
            for y in range(2):
                for d in range(2):
                    if y in halves(k, d):
                        zz = behind(d, k + 1)
                        ring_copy(q, d, k, y, zz).wait_recv()
                        if k < 3 and y in halves(k + 1, d):
                            start(ring_copy(q, d, k + 1, y, zz))
            if k == 3:
                start(sib_copy(q, 7, (z + 4) % 8, c))
            else:
                for d in range(2):
                    start(sib_copy(q, 1 + 2 * k + d, behind(d, k + 1), c))

        for k in range(4):
            for q in range(2):
                arrivals(q, k)
                if k > 0:
                    sib_wait(2 * k - 1 + q, behind(q, k))
                    absorb(behind(q, k))
                elif q == 0:
                    absorb(z)
                else:

                    @pl.when(t > 0)
                    def _():
                        absorb_held(3, 5)

            if k == 1:
                pl.when(t == 0)(lambda: cross_start(0))
            if k == 3:
                pl.when(t == 0)(lambda: pair_start(0))
        pl.when(t < ticks - 1)(lambda: spread_start(t + 1))
        sib_wait(7, (z + 4) % 8)
        absorb((z + 4) % 8)

        def scaled(lo):
            rows = pl.ds(lo, 128)
            r = lax.rsqrt(jnp.sum(ssq[rows, :], axis=1, keepdims=True) / width + EPS)
            gate = jnp.where(r > 0.0, r * acc_g[rows, :], 0.0)
            up = jnp.where(r > 0.0, r * acc_u[rows, :], 0.0)
            return r, gate, up

        def hidden_forward():
            _, gate, up = scaled(0)
            hid[...] = (gate * jax.nn.sigmoid(gate) * up).astype(BF16)

        def hidden_backward():
            r, gate, up = scaled(128)
            sig = jax.nn.sigmoid(gate)
            grad_h = acc_h[...]
            dg = (grad_h * up * sig * (1.0 + gate * (1.0 - sig))).astype(BF16)
            du = (grad_h * gate * sig).astype(BF16)
            dgu[...] = jnp.concatenate([dg, du], axis=1)
            inner = jnp.sum(dg.astype(F32) * gate + du.astype(F32) * up, axis=1, keepdims=True)
            cols[0] = jnp.broadcast_to(r, (128, 128))
            cols[1] = jnp.broadcast_to(inner / width, (128, 128))

        def terms(q, zz, y):
            at = pl.ds(pl.multiple_of((y * 8 + zz) * 256, 256), 256)
            if q == 0:
                return dot(hid[...], wd[:, at])
            dn = dot(dgu[...], wgu[:, at]) * gain[:, at]
            rb = jnp.concatenate([cols[0], cols[0]], axis=1)
            cb = jnp.concatenate([cols[1], cols[1]], axis=1)
            return rb * (dn - held(zz, y).astype(F32) * rb * cb)

        def produce(q, slot, zz):
            def one(y, _):
                value = terms(q, zz, y)
                lo, hi = value[:, :128], value[:, 128:]
                own[q, zz, y] = jnp.where(c == 0, lo, hi)
                sib_out[t, q, zz, y] = jnp.where(c == 0, hi, lo).astype(BF16)
                return 0

            lax.fori_loop(0, 2, one, 0)
            start(
                remote(sib_out.at[t, q, zz], sib_in.at[t, q, zz], rsib_s.at[t, q, slot], rsib_r.at[t, q, slot], sibling)
            )

        def dest(d, k):
            return (z + 4 - k) % 8 if d == 0 else (z + 4 + k) % 8

        def produce_step(q, k):
            if k in (0, 4):
                produce(q, 2 * k - (k > 0), dest(0, k))
            else:
                for d in range(2):
                    produce(q, 2 * k - 1 + d, dest(d, k))

        def sib_ready(q, slot, zz):
            ref = sib_in.at[t, q, zz]
            remote(ref, ref, rsib_s.at[t, q, slot], rsib_r.at[t, q, slot], sibling).wait_recv()

        def local(q, zz, y):
            return own[q, zz, y] + sib_in[t, q, zz, y].astype(F32)

        def ring_sum(q, d, k, y):
            return remote(
                ring_out.at[t, q, d, k, y],
                ring_in.at[t, q, d, k, y],
                rs_s.at[t, q, d, k, y],
                rs_r.at[t, q, d, k, y],
                ring[d],
            )

        def pass_on(q, k):
            if k == 0:
                sib_ready(q, 0, dest(0, 0))
            else:
                for d in range(2):
                    sib_ready(q, 2 * k - 1 + d, dest(d, k))
            for y in range(2):
                for d in range(2):
                    if k == 0 and y != d:
                        continue
                    total = local(q, dest(d, k), y)
                    if k > 1 or (k == 1 and y == d):
                        ring_sum(q, d, k - 1, y).wait_recv()
                        total += ring_in[t, q, d, k - 1, y].astype(F32)
                    ring_out[t, q, d, k, y] = total.astype(BF16)
                    start(ring_sum(q, d, k, y))

        hidden_forward()
        produce_step(0, 0)

        @pl.when(t == 0)
        def _():
            pair(0, 1 - c).wait_recv()
            pair(0, c).wait_send()
            absorb_held(0, 8)

        hidden_backward()
        produce_step(1, 0)
        for k in range(4):
            for q in range(2):
                pass_on(q, k)
                produce_step(q, k + 1)
            if k == 1:
                pl.when(t < ticks - 1)(lambda: cross_start(t + 1))

        def finish(q):
            sib_ready(q, 7, z)
            for y in range(2):
                for d in range(2):
                    ring_sum(q, d, 3, y).wait_recv()

        def summed(q, y):
            total = local(q, z, y) + ring_in[t, q, 0, 3, y].astype(F32) + ring_in[t, q, 1, 3, y].astype(F32)
            return total + jnp.where(y == yh, ag[t, q, c, z, yh].astype(F32), 0.0)

        @pl.when(t < ticks - 1)
        def _():
            for q, edge, fresh, move in ((0, 7, fresh_f, f_move), (1, 0, fresh_b, b_move)):
                finish(q)
                for y in range(2):
                    new = jnp.where(y == yh, fresh[t].astype(F32), 0.0)
                    part_out[t, q, y] = jnp.where(sec == edge, new, summed(q, y)).astype(BF16)
                for y in range(2):
                    move(t, y, yh).start()
            pair_start(t + 1)
            for copy in sends:
                copy.wait_send()
            spread_sent(t + 1)

        @pl.when(t == ticks - 1)
        def _():
            moves = []
            for q in range(2):
                finish(q)
                part_out[t, q, 1 - yh] = summed(q, 1 - yh).astype(BF16)
                copy = remote(
                    part_out.at[t, q, 1 - yh],
                    part_in.at[t, q, yh, 1 - yh],
                    sh_s.at[t, q, 0],
                    sh_r.at[t, q, yh],
                    other_y,
                )
                copy.start()
                moves.append(copy)
            for copy in sends:
                copy.wait_send()
            for q in range(2):
                ref = part_in.at[t, q, 1 - yh, yh]
                remote(ref, ref, sh_s.at[t, q, 0], sh_r.at[t, q, 1 - yh], other_y).wait_recv()
                outs[q] = (summed(q, yh) + part_in[t, q, 1 - yh, yh].astype(F32)).astype(BF16)
            for copy in moves:
                copy.wait_send()

        return 0

    lax.fori_loop(0, ticks, tick, 0)
    for copy in first + stashed:
        copy.wait_send()
    spread_sent(0)


def on_device(act_in, grad_in, fresh_in, fresh_grad, stash, plan, gain, w_gate, w_up, w_down):
    ticks = plan.shape[0]
    rows, cols = act_in.shape[1:]
    width, units = w_gate.shape[1:]
    tile = (rows, cols)
    vmem = pl.BlockSpec(memory_space=pltpu.VMEM)
    anywhere = pl.BlockSpec(memory_space=pl.ANY)
    hbm = pl.BlockSpec(memory_space=pltpu.HBM)
    dma = pltpu.SemaphoreType.DMA
    both = pl.pallas_call(
        functools.partial(kernel, ticks),
        out_shape=jax.ShapeDtypeStruct((2,) + tile, BF16),
        in_specs=[hbm] * 5 + [pl.BlockSpec(memory_space=pltpu.SMEM), hbm] + [anywhere] * 3,
        out_specs=vmem,
        scratch_shapes=[
            pltpu.VMEM(fresh_in.shape, BF16),
            pltpu.VMEM(fresh_grad.shape, BF16),
            pltpu.VMEM(stash.shape[1:], BF16),
            pltpu.VMEM(gain.shape, F32),
            dma((6,)),
            pltpu.VMEM((2 * units, width), BF16),
            pltpu.VMEM((units, width), BF16),
            pltpu.VMEM((ticks, 2, 2, 8, 2) + tile, BF16),
            pltpu.VMEM((ticks, 2, 2, 8) + tile, BF16),
            pltpu.VMEM((ticks,) + tile, BF16),
            pltpu.VMEM((ticks, 2, 8, 2) + tile, BF16),
            pltpu.VMEM((ticks, 2, 8, 2) + tile, BF16),
            pltpu.VMEM((2, 8, 2) + tile, F32),
            pltpu.VMEM((ticks, 2, 2, 4, 2) + tile, BF16),
            pltpu.VMEM((ticks, 2, 2, 4, 2) + tile, BF16),
            pltpu.VMEM((ticks, 2, 2) + tile, BF16),
            pltpu.VMEM((ticks, 2, 2, 2) + tile, BF16),
            pltpu.VMEM((2 * rows, units), F32),
            pltpu.VMEM((2 * rows, units), F32),
            pltpu.VMEM((rows, units), F32),
            pltpu.VMEM((2 * rows, 128), F32),
            pltpu.VMEM((rows, units), BF16),
            pltpu.VMEM((rows, 2 * units), BF16),
            pltpu.VMEM((2, rows, 128), F32),
            dma((3, PARTS)),
            dma((2,)),
            dma((2,)),
            dma((ticks,)),
            dma((ticks,)),
            dma((ticks, 7)),
            dma((ticks, 7)),
            dma((ticks,)),
            dma((ticks,)),
            dma((ticks,)),
            dma((ticks,)),
            dma((ticks, 2, 2, 4, 2)),
            dma((ticks, 2, 2, 4, 2)),
            dma((ticks, 2, 8)),
            dma((ticks, 2, 8)),
            dma((ticks, 2, 8)),
            dma((ticks, 2, 8)),
            dma((ticks, 2, 2, 4, 2)),
            dma((ticks, 2, 2, 4, 2)),
            dma((ticks, 2, 2)),
            dma((ticks, 2, 2)),
        ],
        compiler_params=pltpu.CompilerParams(
            collective_id=0, has_side_effects=True, vmem_limit_bytes=56 * 2**20
        ),
        name="relay",
    )(act_in, grad_in, fresh_in, fresh_grad, stash, plan, gain, jnp.swapaxes(w_gate, 1, 2), jnp.swapaxes(w_up, 1, 2), w_down)
    return both[:1], both[1:]


def solution(mesh):
    in_specs = (
        P("section", None, "tp"),
        P("section", None, "tp"),
        P(None, None, "tp"),
        P(None, None, "tp"),
        P("section", None, None, "tp"),
        P(),
        P("section", None),
        P("section", None, "tp"),
        P("section", None, "tp"),
        P("section", "tp", None),
    )
    out_specs = (P("section", None, "tp"), P("section", None, "tp"))
    return jax.shard_map(on_device, mesh=mesh, in_specs=in_specs, out_specs=out_specs, check_vma=False)
```
